32 devices in a mesh: dp: 2 (over core), mp: 16 (over z, y, x).
Axes of the slice: x: 2, y: 2, z: 4, core: 2. Of those that a mesh axis runs over, the one named last changes fastest.
Arguments:
- rollout_acts: bfloat16 [512, 8192], P(('dp', 'mp')), may hold values from -6 to 6
- gate_pre: bfloat16 [512, 28672], P('dp', 'mp'), may hold values from -6 to 6
- up_pre: bfloat16 [512, 28672], P('dp', 'mp'), may hold values from -6 to 6
- hidden_grad: bfloat16 [512, 28672], P('dp', 'mp'), may hold values from -6 to 6
- row_counts: int32 [2, 16], P('dp'), may hold values from 1 to 16, as said below
- seq_lengths: int32 [2, 4], P('dp'), may hold values from 1 to 112, 224 in all within a row
- tile_owner: int32 [2080], P('mp'), may hold values from 0 to 2079, each once
Outputs:
- act_gram: bfloat16 [2080, 128, 128], P('mp', 'dp')
- grad_gram: bfloat16 [2, 32, 28, 128, 128], P(None, 'mp', None, 'dp')
The draws below stay inside these ranges and needn't reach their ends.
Inputs may be any that keep to these rules, and one draw needn't show every extreme that they name: In group g the live rows fill the first row_counts[g, j] of the 16 slots of device j; row_counts[g, :] sums to exactly 224, and in each group some device has all 16 slots live. seq_lengths[g, :] sums to exactly 224: the live rows of group g, taken by position, are its 4 sequences in order. `tile_owner`: each tile number appears once.
All inputs are finite; a program needn't handle non-finite values.
Results may differ from the reference program's by a relative error of at most 0.0064.
Values may be sent and summed in bfloat16 or wider, within the bound.
A program may use at most 128 MiB of HBM per device.

```python
import math
import jax
import jax.numpy as jnp
import numpy as np
from jax import lax

D = 8192
FF = 28672
TILE = 128
GBLK = 896
CAP = 16
ROWS = 512
LIVE = 224
SEQS = 4
MAXLEN = 112
TRI = 2080
N_DP = 2
N_MP = 16


def draw_row_counts(key, part):
    dead_rows = 2 * CAP
    unit_span = CAP - 1
    unit_total = N_MP * unit_span

    def one_group(group_key):
        full_key, score_key = jax.random.split(group_key)
        keeper = jax.random.randint(full_key, (), 0, N_MP).astype(jnp.int32)
        unit_owner = jnp.arange(unit_total, dtype=jnp.int32) // unit_span
        scores = jax.random.randint(score_key, (unit_total,), 0, 1 << 20).astype(jnp.int32) * unit_total + jnp.arange(unit_total, dtype=jnp.int32)
        scores = jnp.where(unit_owner == keeper, -1, scores)
        chosen = lax.top_k(scores, dead_rows)[1].astype(jnp.int32)
        picked_owner = chosen // unit_span
        device_ids = jnp.arange(N_MP, dtype=jnp.int32)
        deficit = jnp.sum((picked_owner[:, None] == device_ids[None, :]).astype(jnp.int32), axis=0)
        return (CAP - deficit).astype(jnp.int32)
    return jax.vmap(one_group)(jax.random.split(key, N_DP))


def block_levels(own_key, shape, pieces, smallest, top_value):
    def one(dim, shards_of):
        steps = jax.random.uniform(jax.random.fold_in(jax.random.fold_in(own_key, 6), dim), (shards_of,), jnp.float32, smallest / len(pieces), top_value / len(pieces))
        return jnp.repeat(jnp.exp(steps), shape[dim] // shards_of).reshape((-1,) + (1,) * (len(shape) - dim - 1))

    gain = one(*pieces[0])
    for cut in pieces[1:]:
        gain = gain * one(*cut)
    return gain


def split_up(number_of, total, reach, skew):
    loads = [(1 << 20) // math.isqrt(rank ** skew) + 1 for rank in range(2, number_of + 1)]
    spare, given = total - reach - (number_of - 1), [1] * (number_of - 1)
    while spare > 0:
        movable = [i for i in range(number_of - 1) if given[i] < reach]
        mass, remaining = sum([loads[i] for i in movable]), spare
        for i in movable:
            extra = min(reach - given[i], max(1, remaining * loads[i] // mass), spare)
            given[i] = given[i] + extra
            spare = spare - extra
    return np.array([reach] + given)


def uneven(own_key, count, total, bound, skew):
    if count == 2:
        one = jax.random.randint(own_key, (), max(1, total - bound), min(bound, total - 1) + 1)
        return jnp.stack([one, total - one])
    tallies = jnp.asarray(split_up(count, total, bound, skew), jnp.int32)
    couples = (count - 1) // 2
    source_of, sink = tallies[1:1 + 2 * couples:2], tallies[2:2 + 2 * couples:2]
    room = jnp.minimum(source_of - 1, bound - sink)
    moved = jax.random.randint(jax.random.fold_in(own_key, 1), (couples,), 0, 1 << 20) % (room + 1)
    tallies = tallies.at[1:1 + 2 * couples:2].set(source_of - moved).at[2:2 + 2 * couples:2].set(sink + moved)
    return tallies[jax.random.permutation(jax.random.fold_in(own_key, 2), count)]


def scatter_about(key, extent, width, most, cuts=(), kind=jnp.bfloat16):
    entries = jax.random.normal(key, extent, jnp.float32) * width
    if len(cuts) > 0:
        entries = block_levels(key, extent, cuts, -0.22, 0.18) * entries
    return jnp.clip(entries, min=-most, max=most).astype(kind)


def setup_inputs(seed: int = 0) -> dict:
    key_list = jax.random.split(jax.random.key(seed), 8)
    rollout_acts = scatter_about(key_list[0], (ROWS, D), 1.0, 6.0, ((0, 32),))
    gate_pre = scatter_about(key_list[1], (ROWS, FF), 1.0, 6.0, ((0, 2), (1, 16)))
    up_pre = scatter_about(key_list[2], (ROWS, FF), 1.0, 6.0, ((0, 2), (1, 16)))
    hidden_grad = scatter_about(key_list[3], (ROWS, FF), 1.0, 6.0, ((0, 2), (1, 16)))
    row_counts = draw_row_counts(jax.random.fold_in(key_list[7], 71), 0)
    seq_lengths = jax.vmap(lambda own: uneven(own, SEQS, LIVE, MAXLEN, 2))(jax.random.split(key_list[5], N_DP)).reshape((N_DP, SEQS)).astype(jnp.int32)
    tile_owner = jax.random.permutation(key_list[6], TRI).astype(jnp.int32)
    return {"rollout_acts": rollout_acts, "gate_pre": gate_pre, "up_pre": up_pre, "hidden_grad": hidden_grad, "row_counts": row_counts, "seq_lengths": seq_lengths, "tile_owner": tile_owner}


def tile_coords(tile_ids, block_count):
    block_ids = jnp.arange(block_count, dtype=jnp.int32)
    starts = block_ids * block_count - (block_ids * (block_ids - 1)) // 2
    row_block = jnp.sum((tile_ids[:, None] >= starts[None, :]).astype(jnp.int32), axis=1).astype(jnp.int32) - 1
    first_tile = jnp.sum(jnp.where(block_ids[None, :] == row_block[:, None], starts[None, :], 0), axis=1).astype(jnp.int32)
    col_block = tile_ids - first_tile + row_block
    return row_block, col_block


def slot_weights(counts, lengths, capacity, live_total):
    slot_count = counts.shape[0] * capacity
    slot_ids = jnp.arange(slot_count, dtype=jnp.int32)
    device_ids = jnp.arange(counts.shape[0], dtype=jnp.int32)
    owner_match = (slot_ids // capacity)[:, None] == device_ids[None, :]
    within = slot_ids % capacity
    count_here = jnp.sum(jnp.where(owner_match, counts[None, :], 0), axis=1).astype(jnp.int32)
    before = (jnp.cumsum(counts) - counts).astype(jnp.int32)
    offset = jnp.sum(jnp.where(owner_match, before[None, :], 0), axis=1).astype(jnp.int32)
    live_mask = within < count_here
    position = offset + within
    seq_ends = jnp.cumsum(lengths).astype(jnp.int32)
    seq_match = (position[:, None] < seq_ends[None, :]) & (position[:, None] >= (seq_ends - lengths)[None, :])
    own_length = jnp.sum(jnp.where(seq_match, lengths[None, :], 0), axis=1).astype(jnp.int32)
    own_length = jnp.maximum(own_length, 1)
    ratio = live_total / lengths.shape[0]
    weight = jnp.where(live_mask, ratio / own_length.astype(jnp.float32), 0.0).astype(jnp.float32)
    return live_mask, position, weight


def reference(rollout_acts, gate_pre, up_pre, hidden_grad, row_counts, seq_lengths, tile_owner):
    group_rows = N_MP * CAP
    live_total = group_rows - 2 * CAP
    row_scale = 1.0 / (N_DP * live_total)
    live_mask, position, weight = jax.vmap(lambda counts, lengths: slot_weights(counts, lengths, CAP, live_total))(row_counts, seq_lengths)
    acts = rollout_acts.reshape(N_DP, group_rows, D) * live_mask[:, :, None].astype(jnp.bfloat16)
    acts_wide = acts.astype(jnp.float32)
    block_count = D // TILE

    def gram_strip(block_index):
        left_rows = lax.dynamic_slice_in_dim(acts_wide, block_index * TILE, TILE, 2)
        partial_sums = jnp.einsum('gni,gnj->gij', left_rows, acts_wide) * row_scale
        rounded = lax.optimization_barrier(partial_sums.astype(jnp.bfloat16))
        return jnp.sum(rounded.astype(jnp.float32), axis=0).astype(jnp.bfloat16)

    strips = lax.map(gram_strip, jnp.arange(block_count, dtype=jnp.int32))
    tiled = strips.reshape(block_count, TILE, block_count, TILE).transpose(0, 2, 1, 3)
    row_block, col_block = tile_coords(tile_owner, block_count)
    act_gram = tiled[row_block, col_block]

    span = GBLK // TILE
    upper_rows, upper_cols = np.triu_indices(span)
    gate_groups = gate_pre.reshape(N_DP, group_rows, FF)
    up_groups = up_pre.reshape(N_DP, group_rows, FF)
    cot_groups = hidden_grad.reshape(N_DP, group_rows, FF)
    weight_col = weight[:, :, None]

    def gram_block(block_index):
        gate_value = lax.dynamic_slice_in_dim(gate_groups, block_index * GBLK, GBLK, 2).astype(jnp.float32)
        up_value = lax.dynamic_slice_in_dim(up_groups, block_index * GBLK, GBLK, 2).astype(jnp.float32)
        hidden_cot = lax.dynamic_slice_in_dim(cot_groups, block_index * GBLK, GBLK, 2).astype(jnp.float32)
        sigmoid_gate = jax.nn.sigmoid(gate_value)
        gate_grad = hidden_cot * up_value * sigmoid_gate * (1.0 + gate_value * (1.0 - sigmoid_gate))
        up_grad = hidden_cot * gate_value * sigmoid_gate
        scaled_low = lax.optimization_barrier((jnp.stack([gate_grad, up_grad]) * weight_col[None]).astype(jnp.bfloat16))
        scaled = scaled_low.astype(jnp.float32)
        gram_full = jnp.einsum('kgni,kgnj->kgij', scaled, scaled) * row_scale
        rounded = lax.optimization_barrier(gram_full.astype(jnp.bfloat16))
        summed = jnp.sum(rounded.astype(jnp.float32), axis=1).astype(jnp.bfloat16)
        tiles_all = summed.reshape(2, span, TILE, span, TILE).transpose(0, 1, 3, 2, 4)
        return tiles_all[:, upper_rows, upper_cols]

    grads = lax.map(gram_block, jnp.arange(FF // GBLK, dtype=jnp.int32))
    grad_gram = grads.transpose(1, 0, 2, 3, 4)
    return act_gram, grad_gram
```

```python
import functools

import jax
import jax.numpy as jnp
from jax import lax
from jax.experimental import pallas as pl
from jax.experimental.pallas import tpu as pltpu
from jax.sharding import PartitionSpec as P

TILE = 128
GBLK = 896
MESH = pl.DeviceIdType.MESH
F32 = jnp.float32
BF16 = jnp.bfloat16


def largest_divisor(number, limit):
    return max(d for d in range(1, limit + 1) if number % d == 0)


def fused_kernel(
    scale,
    ratio,
    act_in,
    gate_in,
    up_in,
    hid_in,
    counts,
    lengths,
    owner,
    act_out,
    grad_out,
    own_raw,
    gate,
    up,
    hid,
    xs,
    xt,
    sc,
    sct,
    wt,
    rb,
    cb,
    part_a,
    recv_a,
    part_g,
    recv_g,
    stage_a,
    stage_g,
    in_sem,
    out_a_sem,
    out_g_sem,
    zs,
    zr,
    fs,
    fr,
    hs,
    hr,
    gs,
    gr,
    as_,
    ar,
):
    g = lax.axis_index("dp")
    me = lax.axis_index("mp")
    z = me // 4
    y = (me // 2) % 2
    x = me % 2
    xy = me % 4
    xn = me + 1 - 2 * x
    yn = me + 2 - 4 * y
    z1 = z + 1 - 2 * (z % 2)
    z2 = (z + 2) % 4
    z3 = 3 - z
    mid = ((z + 1) // 2) % 2
    is_mid = mid == 1
    zorder = (z, z1, mid * z3 + (1 - mid) * z2, mid * z2 + (1 - mid) * z3)
    cap = act_in.shape[0]
    blocks = xs.shape[1]
    half = blocks // 2
    xy_of_xn = y * 2 + (1 - x)
    xy_of_yn = (1 - y) * 2 + x
    xy_of_d = (1 - y) * 2 + (1 - x)

    loads = [
        pltpu.make_async_copy(act_in, own_raw, in_sem.at[0]),
        pltpu.make_async_copy(gate_in, gate, in_sem.at[1]),
        pltpu.make_async_copy(up_in, up, in_sem.at[2]),
        pltpu.make_async_copy(hid_in, hid, in_sem.at[3]),
    ]
    for copy in loads:
        copy.start()

    loads[0].wait()
    live = counts[0, me]
    row_live = lax.broadcasted_iota(jnp.int32, (cap, TILE), 0) < live

    def put_own(b, carry):
        value = own_raw[:, pl.ds(pl.multiple_of(b * TILE, TILE), TILE)]
        xs[me, b] = jnp.where(row_live, value.astype(F32), 0.0).astype(BF16)
        return carry

    lax.fori_loop(0, blocks, put_own, 0, unroll=8)

    barrier = pltpu.get_barrier_semaphore()
    for other in ((1 - g, me), (g, xn), (g, yn), (g, z1 * 4 + xy)):
        pl.semaphore_signal(barrier, inc=1, device_id=other, device_id_type=MESH)

    @pl.when(is_mid)
    def _():
        pl.semaphore_signal(
            barrier, inc=1, device_id=(g, z3 * 4 + xy), device_id_type=MESH
        )

    pl.semaphore_wait(barrier, 4 + mid)

    def z_copy(src_z, target_z, index, which):
        slot = xs.at[src_z * 4 + xy]
        return pltpu.make_async_remote_copy(
            src_ref=slot, dst_ref=slot, send_sem=zs.at[index], recv_sem=zr.at[which],
            device_id=(g, target_z * 4 + xy), device_id_type=MESH,
        )

    def full_copy(way, item, slot_xy, target):
        slot = xs.at[zorder[item] * 4 + slot_xy]
        return pltpu.make_async_remote_copy(
            src_ref=slot, dst_ref=slot, send_sem=fs.at[way, item], recv_sem=fr.at[way, item],
            device_id=(g, target), device_id_type=MESH,
        )

    def half_copy(way, item, slot_xy, target):
        slot = xs.at[zorder[item] * 4 + slot_xy, pl.ds(way * half, half)]
        return pltpu.make_async_remote_copy(
            src_ref=slot, dst_ref=slot, send_sem=hs.at[way, item], recv_sem=hr.at[way, item],
            device_id=(g, target), device_id_type=MESH,
        )

    def send_item(item):
        full_copy(0, item, xy, xn).start()
        full_copy(1, item, xy, yn).start()

    def pass_halves(item):
        full_copy(1, item, xy_of_yn, yn).wait_recv()
        half_copy(0, item, xy_of_yn, xn).start()
        full_copy(0, item, xy_of_xn, xn).wait_recv()
        half_copy(1, item, xy_of_xn, yn).start()

    def take_halves(item):
        half_copy(0, item, xy_of_d, xn).wait_recv()
        half_copy(1, item, xy_of_d, yn).wait_recv()

    z_copy(z, z1, 0, 0).start()
    send_item(0)

    @pl.when(is_mid)
    def _():
        z_copy(z, z3, 1, 1).start()

    within = lax.broadcasted_iota(jnp.int32, (cap, TILE), 0)
    seqs = lengths.shape[1]

    def put_weight(j, offset):
        here = counts[0, j]
        position = within + offset
        own = jnp.ones((cap, TILE), jnp.int32)
        start = jnp.int32(0)
        for k in range(seqs):
            size = lengths[0, k]
            inside = (position >= start) & (position < start + size)
            own = jnp.where(inside, size, own)
            start = start + size
        own = jnp.maximum(own, 1).astype(F32)
        wt[pl.ds(pl.multiple_of(j * cap, cap), cap), :] = jnp.where(
            within < here, ratio / own, 0.0
        )
        return offset + here

    lax.fori_loop(0, counts.shape[1], put_weight, jnp.int32(0))

    for copy in loads[1:]:
        copy.wait()
    per = sc.shape[1]
    span = GBLK // TILE
    rows = gate.shape[0]
    chunk = 64

    def scaled_block(n, carry):
        m = n // span
        for c in range(rows // chunk):
            rs = slice(c * chunk, (c + 1) * chunk)
            cols = pl.ds(pl.multiple_of(n * TILE, TILE), TILE)
            a = gate[rs, cols].astype(F32)
            b = up[rs, cols].astype(F32)
            h = hid[rs, cols].astype(F32)
            w = wt[rs, :]
            q = 0.5 * jnp.tanh(0.5 * a) + 0.5
            hq = h * q
            gate_grad = hq * b * (1.0 + a * (1.0 - q))
            up_grad = hq * a
            sc[0, m, n % span, rs, :] = (gate_grad * w).astype(BF16)
            sc[1, m, n % span, rs, :] = (up_grad * w).astype(BF16)
        for e in range(2):
            sct[e, m, n % span] = sc[e, m, n % span].T
        return carry

    lax.fori_loop(0, per * span, scaled_block, 0)

    z_copy(z1, z1, 0, 0).wait_recv()
    send_item(1)

    @pl.when(is_mid)
    def _():
        z_copy(z1, z3, 2, 2).start()

    pass_halves(0)

    pairs = [(i, j) for i in range(span) for j in range(i, span)]
    other_rows = pl.ds(pl.multiple_of(64 * (1 - g), 64), 64)
    own_rows = pl.ds(pl.multiple_of(64 * g, 64), 64)

    def grad_send(q):
        return pltpu.make_async_remote_copy(
            src_ref=part_g.at[q, :, other_rows], dst_ref=recv_g.at[q],
            send_sem=gs.at[q], recv_sem=gr.at[q],
            device_id=(1 - g, me), device_id_type=MESH,
        )

    def grad_tiles(q, carry):
        e = q // per
        m = q % per
        for k, (i, j) in enumerate(pairs):
            tile = jnp.dot(sct[e, m, i], sc[e, m, j], preferred_element_type=F32)
            part_g[q, k] = (tile * scale).astype(BF16)
        grad_send(q).start()
        return carry

    lax.fori_loop(0, 2 * per, grad_tiles, 0)

    z_copy(zorder[2], z1, 0, 1).wait_recv()
    send_item(2)

    @pl.when(is_mid)
    def _():
        z_copy(z3, z1, 1 + 2, 1).start()

    pass_halves(1)

    z_copy(zorder[3], z1, 0, 2).wait_recv()
    send_item(3)

    @pl.when(is_mid)
    def _():
        z_copy(z2, z1, 4, 2).start()

    tiles = owner.shape[0]

    def put_coords(k, carry):
        t = owner[k]
        r = jnp.int32(0)
        step = 1
        while step * 2 < blocks:
            step *= 2
        while step:
            cand = r + step
            begin = cand * blocks - (cand * (cand - 1)) // 2
            r = jnp.where((cand < blocks) & (t >= begin), cand, r)
            step //= 2
        rb[k] = r
        cb[k] = t - (r * blocks - (r * (r - 1)) // 2) + r
        return carry

    lax.fori_loop(0, tiles, put_coords, 0)

    def grad_out_copy(q):
        return pltpu.make_async_copy(
            stage_g.at[q], grad_out.at[q // per, q % per], out_g_sem.at[q]
        )

    def grad_finish(q, carry):
        grad_send(q).wait()
        for k in range(len(pairs)):
            total = part_g[q, k, own_rows].astype(F32) + recv_g[q, k].astype(F32)
            stage_g[q, k] = total.astype(BF16)
        grad_out_copy(q).start()
        return carry

    take_halves(0)
    take_halves(1)

    group = 8

    def transpose_half(which):
        def one(b, carry):
            block = xs[pl.ds(which * group, group), b].reshape(group * cap, TILE)
            xt[b, :, pl.ds(pl.multiple_of(which * TILE, TILE), TILE)] = block.T
            return carry

        lax.fori_loop(0, blocks, one, 0, unroll=4)

    pass_halves(2)
    lax.fori_loop(0, 2 * per, grad_finish, 0)
    pass_halves(3)
    take_halves(2)
    take_halves(3)
    transpose_half(0)
    transpose_half(1)

    chunks = part_a.shape[0]
    width = part_a.shape[1]

    def act_send(n):
        return pltpu.make_async_remote_copy(
            src_ref=part_a.at[n, :, other_rows], dst_ref=recv_a.at[n],
            send_sem=as_.at[n], recv_sem=ar.at[n],
            device_id=(1 - g, me), device_id_type=MESH,
        )

    def act_out_copy(n):
        return pltpu.make_async_copy(
            stage_a.at[n], act_out.at[pl.ds(n * width, width)], out_a_sem.at[n]
        )

    def act_tiles(n, carry):
        for i in range(width):
            k = n * width + i
            left = xt[rb[k]]
            right = xs[:, cb[k]].reshape(2 * TILE, TILE)
            tile = jnp.dot(left, right, preferred_element_type=F32)
            part_a[n, i] = (tile * scale).astype(BF16)
        act_send(n).start()
        return carry

    def act_finish(n, carry):
        act_send(n).wait()
        for i in range(width):
            total = part_a[n, i, own_rows].astype(F32) + recv_a[n, i].astype(F32)
            stage_a[n, i] = total.astype(BF16)
        act_out_copy(n).start()
        return carry

    def act_both(n, carry):
        act_tiles(n, carry)
        act_finish(n - 2, carry)
        return carry

    lax.fori_loop(0, 2, act_tiles, 0)
    lax.fori_loop(2, chunks, act_both, 0)
    lax.fori_loop(chunks - 2, chunks, act_finish, 0)

    z_copy(z, z1, 0, 0).wait_send()

    @pl.when(is_mid)
    def _():
        z_copy(z, z3, 1, 1).wait_send()
        z_copy(z1, z3, 2, 2).wait_send()
        z_copy(z3, z1, 3, 1).wait_send()
        z_copy(z2, z1, 4, 2).wait_send()

    for item in range(4):
        full_copy(0, item, xy, xn).wait_send()
        full_copy(1, item, xy, yn).wait_send()
        half_copy(0, item, xy_of_yn, xn).wait_send()
        half_copy(1, item, xy_of_xn, yn).wait_send()

    def wait_grad_out(q, carry):
        grad_out_copy(q).wait()
        return carry

    def wait_act_out(n, carry):
        act_out_copy(n).wait()
        return carry

    lax.fori_loop(0, 2 * per, wait_grad_out, 0)
    lax.fori_loop(0, chunks, wait_act_out, 0)


def fused_body(acts, gate, up, hid, counts, lengths, owner):
    cap, width = acts.shape
    slots = 16
    rows = slots * cap
    live_total = rows - 2 * cap
    blocks = width // TILE
    tiles = owner.shape[0]
    per = gate.shape[1] // GBLK
    span = GBLK // TILE
    pairs = span * (span + 1) // 2
    chunk = largest_divisor(tiles, 10)
    chunks = tiles // chunk
    anywhere = pl.BlockSpec(memory_space=pl.ANY)
    smem = pl.BlockSpec(memory_space=pltpu.SMEM)
    dma = pltpu.SemaphoreType.DMA
    kernel = functools.partial(
        fused_kernel, 1.0 / (2 * live_total), live_total / lengths.shape[1]
    )
    return pl.pallas_call(
        kernel,
        out_shape=(
            jax.ShapeDtypeStruct((tiles, TILE // 2, TILE), BF16),
            jax.ShapeDtypeStruct((2, per, pairs, TILE // 2, TILE), BF16),
        ),
        in_specs=[anywhere] * 4 + [smem] * 3,
        out_specs=(anywhere, anywhere),
        scratch_shapes=[
            pltpu.VMEM((cap, width), BF16),
            pltpu.VMEM(gate.shape, BF16),
            pltpu.VMEM(gate.shape, BF16),
            pltpu.VMEM(gate.shape, BF16),
            pltpu.VMEM((slots, blocks, cap, TILE), BF16),
            pltpu.VMEM((blocks, TILE, rows), BF16),
            pltpu.VMEM((2, per, span, rows, TILE), BF16),
            pltpu.VMEM((2, per, span, TILE, rows), BF16),
            pltpu.VMEM((rows, TILE), F32),
            pltpu.SMEM((tiles,), jnp.int32),
            pltpu.SMEM((tiles,), jnp.int32),
            pltpu.VMEM((chunks, chunk, TILE, TILE), BF16),
            pltpu.VMEM((chunks, chunk, TILE // 2, TILE), BF16),
            pltpu.VMEM((2 * per, pairs, TILE, TILE), BF16),
            pltpu.VMEM((2 * per, pairs, TILE // 2, TILE), BF16),
            pltpu.VMEM((chunks, chunk, TILE // 2, TILE), BF16),
            pltpu.VMEM((2 * per, pairs, TILE // 2, TILE), BF16),
            dma((4,)),
            dma((chunks,)),
            dma((2 * per,)),
            dma((5,)),
            dma((3,)),
            dma((2, 4)),
            dma((2, 4)),
            dma((2, 4)),
            dma((2, 4)),
            dma((2 * per,)),
            dma((2 * per,)),
            dma((chunks,)),
            dma((chunks,)),
        ],
        compiler_params=pltpu.CompilerParams(
            collective_id=0, has_side_effects=True, vmem_limit_bytes=50 * 2**20
        ),
        cost_estimate=pl.CostEstimate(
            flops=4 * 10**9, bytes_accessed=12 * 10**6, transcendentals=10**6
        ),
    )(acts, gate, up, hid, counts, lengths, owner)


def tile_coords(tile_ids, block_count):
    block_ids = jnp.arange(block_count, dtype=jnp.int32)
    starts = block_ids * block_count - block_ids * (block_ids - 1) // 2
    row_block = jnp.sum((tile_ids[:, None] >= starts[None, :]).astype(jnp.int32), axis=1) - 1
    first_tile = jnp.sum(
        jnp.where(block_ids[None, :] == row_block[:, None], starts[None, :], 0), axis=1
    )
    return row_block, tile_ids - first_tile + row_block


def sums_before(values):
    ids = jnp.arange(values.shape[0], dtype=jnp.int32)
    return jnp.sum(jnp.where(ids[None, :] < ids[:, None], values[None, :], 0), axis=1)


def slot_weights(counts, lengths, capacity, live_total):
    slot_ids = jnp.arange(counts.shape[0] * capacity, dtype=jnp.int32)
    device_ids = jnp.arange(counts.shape[0], dtype=jnp.int32)
    match = (slot_ids // capacity)[:, None] == device_ids[None, :]
    within = slot_ids % capacity
    live_mask = within < jnp.sum(jnp.where(match, counts[None, :], 0), axis=1)
    position = within + jnp.sum(jnp.where(match, sums_before(counts)[None, :], 0), axis=1)
    begins = sums_before(lengths)
    inside = (position[:, None] >= begins[None, :]) & (
        position[:, None] < (begins + lengths)[None, :]
    )
    own = jnp.maximum(jnp.sum(jnp.where(inside, lengths[None, :], 0), axis=1), 1)
    ratio = live_total / lengths.shape[0]
    return live_mask, jnp.where(live_mask, ratio / own.astype(F32), 0.0)


def general_body(acts, gate_pre, up_pre, hidden_grad, counts, lengths, owner):
    mp_size = lax.axis_size("mp")
    dp_size = lax.axis_size("dp")
    capacity = acts.shape[0]
    live_total = mp_size * capacity - 2 * capacity
    scale = 1.0 / (dp_size * live_total)
    live_mask, weight = slot_weights(counts[0], lengths[0], capacity, live_total)
    row_block, col_block = tile_coords(owner, acts.shape[1] // TILE)
    a = gate_pre.astype(F32)
    b = up_pre.astype(F32)
    h = hidden_grad.astype(F32)
    q = jax.nn.sigmoid(a)
    w = weight[:, None]
    scaled = (
        (h * b * q * (1.0 + a * (1.0 - q)) * w).astype(BF16),
        (h * a * q * w).astype(BF16),
    )
    per = gate_pre.shape[1] // GBLK
    span = GBLK // TILE
    pieces = []
    for e in range(2):
        for block in range(per):
            for strip in range(span):
                first = block * GBLK + strip * TILE
                product = lax.dot_general(
                    scaled[e][:, first : first + TILE],
                    scaled[e][:, first : (block + 1) * GBLK],
                    (((0,), (0,)), ((), ())),
                    preferred_element_type=F32,
                )
                product = (product * scale).astype(BF16)
                pieces.append(product.reshape(TILE, span - strip, TILE).transpose(1, 0, 2))
    grad_tiles = jnp.concatenate(pieces, axis=0)
    mine = jnp.sum(
        jnp.where(
            jnp.arange(mp_size) == lax.axis_index("mp"), counts[0], 0
        )
    )
    kept = jnp.where(jnp.arange(capacity)[:, None] < mine, acts, 0)
    rows = lax.all_gather(kept, "mp", axis=0, tiled=True)

    def one_tile(pair):
        left = lax.dynamic_slice_in_dim(rows, pair[0] * TILE, TILE, 1)
        right = lax.dynamic_slice_in_dim(rows, pair[1] * TILE, TILE, 1)
        product = lax.dot_general(
            left, right, (((0,), (0,)), ((), ())), preferred_element_type=F32
        )
        return (product * scale).astype(BF16)

    act_tiles = lax.map(one_tile, (row_block, col_block))
    act_gram = lax.psum_scatter(act_tiles, "dp", scatter_dimension=1, tiled=True)
    grad_gram = lax.psum_scatter(grad_tiles, "dp", scatter_dimension=1, tiled=True)
    return act_gram, grad_gram.reshape(2, per, -1, grad_gram.shape[1], TILE)


def solution(mesh):
    fits = mesh.shape["dp"] == 2 and mesh.shape["mp"] == 16
    return jax.shard_map(
        fused_body if fits else general_body,
        mesh=mesh,
        in_specs=(
            P(("dp", "mp"), None),
            P("dp", "mp"),
            P("dp", "mp"),
            P("dp", "mp"),
            P("dp", None),
            P("dp", None),
            P("mp"),
        ),
        out_specs=(P("mp", "dp", None), P(None, "mp", None, "dp", None)),
        check_vma=False,
    )
```

```python
import functools

import jax
import jax.numpy as jnp
from jax import lax
from jax.experimental import pallas as pl
from jax.experimental.pallas import tpu as pltpu
from jax.sharding import PartitionSpec as P

TILE = 128
GBLK = 896
MESH = pl.DeviceIdType.MESH
F32 = jnp.float32
BF16 = jnp.bfloat16


def largest_divisor(number, limit):
    return max(d for d in range(1, limit + 1) if number % d == 0)


def fused_kernel(
    scale,
    ratio,
    act_in,
    gate_in,
    up_in,
    hid_in,
    counts_in,
    lengths_in,
    owner_in,
    act_out,
    grad_out,
    counts,
    lengths,
    owner,
    own_raw,
    gate,
    up,
    hid,
    xs,
    xt,
    sc,
    sct,
    wt,
    rb,
    cb,
    part_a,
    recv_a,
    part_g,
    recv_g,
    stage_a,
    stage_g,
    in_sem,
    out_a_sem,
    out_g_sem,
    zs,
    zr,
    fs,
    fr,
    hs,
    hr,
    gs,
    gr,
    as_,
    ar,
):
    g = lax.axis_index("dp")
    me = lax.axis_index("mp")
    z = me // 4
    y = (me // 2) % 2
    x = me % 2
    xy = me % 4
    xn = me + 1 - 2 * x
    yn = me + 2 - 4 * y
    z1 = z + 1 - 2 * (z % 2)
    z2 = (z + 2) % 4
    z3 = 3 - z
    mid = ((z + 1) // 2) % 2
    is_mid = mid == 1
    zorder = (z, z1, mid * z3 + (1 - mid) * z2, mid * z2 + (1 - mid) * z3)
    cap = act_in.shape[0]
    blocks = xs.shape[1]
    half = blocks // 2
    xy_of_xn = y * 2 + (1 - x)
    xy_of_yn = (1 - y) * 2 + x
    xy_of_d = (1 - y) * 2 + (1 - x)

    loads = [
        pltpu.make_async_copy(counts_in, counts, in_sem.at[4]),
        pltpu.make_async_copy(act_in, own_raw, in_sem.at[0]),
        pltpu.make_async_copy(gate_in, gate, in_sem.at[1]),
        pltpu.make_async_copy(up_in, up, in_sem.at[2]),
        pltpu.make_async_copy(hid_in, hid, in_sem.at[3]),
        pltpu.make_async_copy(lengths_in, lengths, in_sem.at[5]),
        pltpu.make_async_copy(owner_in, owner, in_sem.at[6]),
    ]
    for copy in loads:
        copy.start()

    loads[0].wait()
    loads[1].wait()
    live = counts[0, me]
    row_live = lax.broadcasted_iota(jnp.int32, (cap, TILE), 0) < live

    def put_own(b, carry):
        value = own_raw[:, pl.ds(pl.multiple_of(b * TILE, TILE), TILE)]
        xs[me, b] = jnp.where(row_live, value.astype(F32), 0.0).astype(BF16)
        return carry

    lax.fori_loop(0, blocks, put_own, 0, unroll=8)

    barrier = pltpu.get_barrier_semaphore()
    for other in ((1 - g, me), (g, xn), (g, yn), (g, z1 * 4 + xy)):
        pl.semaphore_signal(barrier, inc=1, device_id=other, device_id_type=MESH)

    @pl.when(is_mid)
    def _():
        pl.semaphore_signal(
            barrier, inc=1, device_id=(g, z3 * 4 + xy), device_id_type=MESH
        )

    pl.semaphore_wait(barrier, 4 + mid)

    def z_copy(src_z, target_z, index, which):
        slot = xs.at[src_z * 4 + xy]
        return pltpu.make_async_remote_copy(
            src_ref=slot, dst_ref=slot, send_sem=zs.at[index], recv_sem=zr.at[which],
            device_id=(g, target_z * 4 + xy), device_id_type=MESH,
        )

    def full_copy(way, item, slot_xy, target):
        slot = xs.at[zorder[item] * 4 + slot_xy]
        return pltpu.make_async_remote_copy(
            src_ref=slot, dst_ref=slot, send_sem=fs.at[way, item], recv_sem=fr.at[way, item],
            device_id=(g, target), device_id_type=MESH,
        )

    def half_copy(way, item, slot_xy, target):
        slot = xs.at[zorder[item] * 4 + slot_xy, pl.ds(way * half, half)]
        return pltpu.make_async_remote_copy(
            src_ref=slot, dst_ref=slot, send_sem=hs.at[way, item], recv_sem=hr.at[way, item],
            device_id=(g, target), device_id_type=MESH,
        )

    def send_item(item):
        full_copy(0, item, xy, xn).start()
        full_copy(1, item, xy, yn).start()

    def pass_halves(item):
        full_copy(1, item, xy_of_yn, yn).wait_recv()
        half_copy(0, item, xy_of_yn, xn).start()
        full_copy(0, item, xy_of_xn, xn).wait_recv()
        half_copy(1, item, xy_of_xn, yn).start()

    def take_halves(item):
        half_copy(0, item, xy_of_d, xn).wait_recv()
        half_copy(1, item, xy_of_d, yn).wait_recv()

    z_copy(z, z1, 0, 0).start()
    send_item(0)

    @pl.when(is_mid)
    def _():
        z_copy(z, z3, 1, 1).start()

    for copy in loads[2:]:
        copy.wait()

    within = lax.broadcasted_iota(jnp.int32, (cap, TILE), 0)
    seqs = lengths.shape[1]

    def put_weight(j, offset):
        here = counts[0, j]
        position = within + offset
        own = jnp.ones((cap, TILE), jnp.int32)
        start = jnp.int32(0)
        for k in range(seqs):
            size = lengths[0, k]
            inside = (position >= start) & (position < start + size)
            own = jnp.where(inside, size, own)
            start = start + size
        own = jnp.maximum(own, 1).astype(F32)
        wt[pl.ds(pl.multiple_of(j * cap, cap), cap), :] = jnp.where(
            within < here, ratio / own, 0.0
        )
        return offset + here

    lax.fori_loop(0, counts.shape[1], put_weight, jnp.int32(0))

    per = sc.shape[1]
    span = GBLK // TILE
    rows = gate.shape[0]
    chunk = 64

    def scaled_block(n, carry):
        m = n // span
        for c in range(rows // chunk):
            rs = slice(c * chunk, (c + 1) * chunk)
            cols = pl.ds(pl.multiple_of(n * TILE, TILE), TILE)
            a = gate[rs, cols].astype(F32)
            b = up[rs, cols].astype(F32)
            h = hid[rs, cols].astype(F32)
            w = wt[rs, :]
            q = 0.5 * jnp.tanh(0.5 * a) + 0.5
            hq = h * q
            gate_grad = hq * b * (1.0 + a * (1.0 - q))
            up_grad = hq * a
            sc[0, m, n % span, rs, :] = (gate_grad * w).astype(BF16)
            sc[1, m, n % span, rs, :] = (up_grad * w).astype(BF16)
        for e in range(2):
            sct[e, m, n % span] = sc[e, m, n % span].T
        return carry

    lax.fori_loop(0, per * span, scaled_block, 0)

    z_copy(z1, z1, 0, 0).wait_recv()
    send_item(1)

    @pl.when(is_mid)
    def _():
        z_copy(z1, z3, 2, 2).start()

    pass_halves(0)

    pairs = [(i, j) for i in range(span) for j in range(i, span)]
    other_rows = pl.ds(pl.multiple_of(64 * (1 - g), 64), 64)
    own_rows = pl.ds(pl.multiple_of(64 * g, 64), 64)

    def grad_send(q):
        return pltpu.make_async_remote_copy(
            src_ref=part_g.at[q, :, other_rows], dst_ref=recv_g.at[q],
            send_sem=gs.at[q], recv_sem=gr.at[q],
            device_id=(1 - g, me), device_id_type=MESH,
        )

    def grad_tiles(q, carry):
        e = q // per
        m = q % per
        for k, (i, j) in enumerate(pairs):
            tile = jnp.dot(sct[e, m, i], sc[e, m, j], preferred_element_type=F32)
            part_g[q, k] = (tile * scale).astype(BF16)
        grad_send(q).start()
        return carry

    lax.fori_loop(0, 2 * per, grad_tiles, 0)

    z_copy(zorder[2], z1, 0, 1).wait_recv()
    send_item(2)

    @pl.when(is_mid)
    def _():
        z_copy(z3, z1, 1 + 2, 1).start()

    pass_halves(1)

    z_copy(zorder[3], z1, 0, 2).wait_recv()
    send_item(3)

    @pl.when(is_mid)
    def _():
        z_copy(z2, z1, 4, 2).start()

    tiles = owner.shape[0]

    def put_coords(k, carry):
        t = owner[k]
        r = jnp.int32(0)
        step = 1
        while step * 2 < blocks:
            step *= 2
        while step:
            cand = r + step
            begin = cand * blocks - (cand * (cand - 1)) // 2
            r = jnp.where((cand < blocks) & (t >= begin), cand, r)
            step //= 2
        rb[k] = r
        cb[k] = t - (r * blocks - (r * (r - 1)) // 2) + r
        return carry

    lax.fori_loop(0, tiles, put_coords, 0)

    def grad_out_copy(q):
        return pltpu.make_async_copy(
            stage_g.at[q], grad_out.at[q // per, q % per], out_g_sem.at[q]
        )

    def grad_finish(q, carry):
        grad_send(q).wait()
        for k in range(len(pairs)):
            total = part_g[q, k, own_rows].astype(F32) + recv_g[q, k].astype(F32)
            stage_g[q, k] = total.astype(BF16)
        grad_out_copy(q).start()
        return carry

    take_halves(0)
    take_halves(1)

    group = 8

    def transpose_half(which):
        def one(b, carry):
            block = xs[pl.ds(which * group, group), b].reshape(group * cap, TILE)
            xt[b, :, pl.ds(pl.multiple_of(which * TILE, TILE), TILE)] = block.T
            return carry

        lax.fori_loop(0, blocks, one, 0, unroll=4)

    pass_halves(2)
    lax.fori_loop(0, 2 * per, grad_finish, 0)
    pass_halves(3)
    take_halves(2)
    take_halves(3)
    transpose_half(0)
    transpose_half(1)

    chunks = part_a.shape[0]
    width = part_a.shape[1]

    def act_send(n):
        return pltpu.make_async_remote_copy(
            src_ref=part_a.at[n, :, other_rows], dst_ref=recv_a.at[n],
            send_sem=as_.at[n], recv_sem=ar.at[n],
            device_id=(1 - g, me), device_id_type=MESH,
        )

    def act_out_copy(n):
        return pltpu.make_async_copy(
            stage_a.at[n], act_out.at[pl.ds(n * width, width)], out_a_sem.at[n]
        )

    def act_tiles(n, carry):
        for i in range(width):
            k = n * width + i
            left = xt[rb[k]]
            right = xs[:, cb[k]].reshape(2 * TILE, TILE)
            tile = jnp.dot(left, right, preferred_element_type=F32)
            part_a[n, i] = (tile * scale).astype(BF16)
        act_send(n).start()
        return carry

    def act_finish(n, carry):
        act_send(n).wait()
        for i in range(width):
            total = part_a[n, i, own_rows].astype(F32) + recv_a[n, i].astype(F32)
            stage_a[n, i] = total.astype(BF16)
        act_out_copy(n).start()
        return carry

    def act_both(n, carry):
        act_tiles(n, carry)
        act_finish(n - 2, carry)
        return carry

    lax.fori_loop(0, 2, act_tiles, 0)
    lax.fori_loop(2, chunks, act_both, 0)
    lax.fori_loop(chunks - 2, chunks, act_finish, 0)

    z_copy(z, z1, 0, 0).wait_send()

    @pl.when(is_mid)
    def _():
        z_copy(z, z3, 1, 1).wait_send()
        z_copy(z1, z3, 2, 2).wait_send()
        z_copy(z3, z1, 3, 1).wait_send()
        z_copy(z2, z1, 4, 2).wait_send()

    for item in range(4):
        full_copy(0, item, xy, xn).wait_send()
        full_copy(1, item, xy, yn).wait_send()
        half_copy(0, item, xy_of_yn, xn).wait_send()
        half_copy(1, item, xy_of_xn, yn).wait_send()

    def wait_grad_out(q, carry):
        grad_out_copy(q).wait()
        return carry

    def wait_act_out(n, carry):
        act_out_copy(n).wait()
        return carry

    lax.fori_loop(0, 2 * per, wait_grad_out, 0)
    lax.fori_loop(0, chunks, wait_act_out, 0)


def fused_body(acts, gate, up, hid, counts, lengths, owner):
    cap, width = acts.shape
    slots = 16
    rows = slots * cap
    live_total = rows - 2 * cap
    blocks = width // TILE
    tiles = owner.shape[0]
    per = gate.shape[1] // GBLK
    span = GBLK // TILE
    pairs = span * (span + 1) // 2
    chunk = largest_divisor(tiles, 10)
    chunks = tiles // chunk
    anywhere = pl.BlockSpec(memory_space=pl.ANY)
    in_hbm = pl.BlockSpec(memory_space=pltpu.HBM)
    dma = pltpu.SemaphoreType.DMA
    kernel = functools.partial(
        fused_kernel, 1.0 / (2 * live_total), live_total / lengths.shape[1]
    )
    return pl.pallas_call(
        kernel,
        out_shape=(
            jax.ShapeDtypeStruct((tiles, TILE // 2, TILE), BF16),
            jax.ShapeDtypeStruct((2, per, pairs, TILE // 2, TILE), BF16),
        ),
        in_specs=[in_hbm] * 7,
        out_specs=(anywhere, anywhere),
        scratch_shapes=[
            pltpu.SMEM(counts.shape, jnp.int32),
            pltpu.SMEM(lengths.shape, jnp.int32),
            pltpu.SMEM(owner.shape, jnp.int32),
            pltpu.VMEM((cap, width), BF16),
            pltpu.VMEM(gate.shape, BF16),
            pltpu.VMEM(gate.shape, BF16),
            pltpu.VMEM(gate.shape, BF16),
            pltpu.VMEM((slots, blocks, cap, TILE), BF16),
            pltpu.VMEM((blocks, TILE, rows), BF16),
            pltpu.VMEM((2, per, span, rows, TILE), BF16),
            pltpu.VMEM((2, per, span, TILE, rows), BF16),
            pltpu.VMEM((rows, TILE), F32),
            pltpu.SMEM((tiles,), jnp.int32),
            pltpu.SMEM((tiles,), jnp.int32),
            pltpu.VMEM((chunks, chunk, TILE, TILE), BF16),
            pltpu.VMEM((chunks, chunk, TILE // 2, TILE), BF16),
            pltpu.VMEM((2 * per, pairs, TILE, TILE), BF16),
            pltpu.VMEM((2 * per, pairs, TILE // 2, TILE), BF16),
            pltpu.VMEM((chunks, chunk, TILE // 2, TILE), BF16),
            pltpu.VMEM((2 * per, pairs, TILE // 2, TILE), BF16),
            dma((7,)),
            dma((chunks,)),
            dma((2 * per,)),
            dma((5,)),
            dma((3,)),
            dma((2, 4)),
            dma((2, 4)),
            dma((2, 4)),
            dma((2, 4)),
            dma((2 * per,)),
            dma((2 * per,)),
            dma((chunks,)),
            dma((chunks,)),
        ],
        compiler_params=pltpu.CompilerParams(
            collective_id=0, has_side_effects=True, vmem_limit_bytes=36 * 2**20
        ),
        cost_estimate=pl.CostEstimate(
            flops=4 * 10**9, bytes_accessed=12 * 10**6, transcendentals=10**6
        ),
    )(
        *(
            pltpu.with_memory_space_constraint(array, pltpu.HBM)
            for array in (acts, gate, up, hid, counts, lengths, owner)
        )
    )


def tile_coords(tile_ids, block_count):
    block_ids = jnp.arange(block_count, dtype=jnp.int32)
    starts = block_ids * block_count - block_ids * (block_ids - 1) // 2
    row_block = jnp.sum((tile_ids[:, None] >= starts[None, :]).astype(jnp.int32), axis=1) - 1
    first_tile = jnp.sum(
        jnp.where(block_ids[None, :] == row_block[:, None], starts[None, :], 0), axis=1
    )
    return row_block, tile_ids - first_tile + row_block


def sums_before(values):
    ids = jnp.arange(values.shape[0], dtype=jnp.int32)
    return jnp.sum(jnp.where(ids[None, :] < ids[:, None], values[None, :], 0), axis=1)


def slot_weights(counts, lengths, capacity, live_total):
    slot_ids = jnp.arange(counts.shape[0] * capacity, dtype=jnp.int32)
    device_ids = jnp.arange(counts.shape[0], dtype=jnp.int32)
    match = (slot_ids // capacity)[:, None] == device_ids[None, :]
    within = slot_ids % capacity
    live_mask = within < jnp.sum(jnp.where(match, counts[None, :], 0), axis=1)
    position = within + jnp.sum(jnp.where(match, sums_before(counts)[None, :], 0), axis=1)
    begins = sums_before(lengths)
    inside = (position[:, None] >= begins[None, :]) & (
        position[:, None] < (begins + lengths)[None, :]
    )
    own = jnp.maximum(jnp.sum(jnp.where(inside, lengths[None, :], 0), axis=1), 1)
    ratio = live_total / lengths.shape[0]
    return live_mask, jnp.where(live_mask, ratio / own.astype(F32), 0.0)


def general_body(acts, gate_pre, up_pre, hidden_grad, counts, lengths, owner):
    mp_size = lax.axis_size("mp")
    dp_size = lax.axis_size("dp")
    capacity = acts.shape[0]
    live_total = mp_size * capacity - 2 * capacity
    scale = 1.0 / (dp_size * live_total)
    live_mask, weight = slot_weights(counts[0], lengths[0], capacity, live_total)
    row_block, col_block = tile_coords(owner, acts.shape[1] // TILE)
    a = gate_pre.astype(F32)
    b = up_pre.astype(F32)
    h = hidden_grad.astype(F32)
    q = jax.nn.sigmoid(a)
    w = weight[:, None]
    scaled = (
        (h * b * q * (1.0 + a * (1.0 - q)) * w).astype(BF16),
        (h * a * q * w).astype(BF16),
    )
    per = gate_pre.shape[1] // GBLK
    span = GBLK // TILE
    pieces = []
    for e in range(2):
        for block in range(per):
            for strip in range(span):
                first = block * GBLK + strip * TILE
                product = lax.dot_general(
                    scaled[e][:, first : first + TILE],
                    scaled[e][:, first : (block + 1) * GBLK],
                    (((0,), (0,)), ((), ())),
                    preferred_element_type=F32,
                )
                product = (product * scale).astype(BF16)
                pieces.append(product.reshape(TILE, span - strip, TILE).transpose(1, 0, 2))
    grad_tiles = jnp.concatenate(pieces, axis=0)
    mine = jnp.sum(
        jnp.where(
            jnp.arange(mp_size) == lax.axis_index("mp"), counts[0], 0
        )
    )
    kept = jnp.where(jnp.arange(capacity)[:, None] < mine, acts, 0)
    rows = lax.all_gather(kept, "mp", axis=0, tiled=True)

    def one_tile(pair):
        left = lax.dynamic_slice_in_dim(rows, pair[0] * TILE, TILE, 1)
        right = lax.dynamic_slice_in_dim(rows, pair[1] * TILE, TILE, 1)
        product = lax.dot_general(
            left, right, (((0,), (0,)), ((), ())), preferred_element_type=F32
        )
        return (product * scale).astype(BF16)

    act_tiles = lax.map(one_tile, (row_block, col_block))
    act_gram = lax.psum_scatter(act_tiles, "dp", scatter_dimension=1, tiled=True)
    grad_gram = lax.psum_scatter(grad_tiles, "dp", scatter_dimension=1, tiled=True)
    return act_gram, grad_gram.reshape(2, per, -1, grad_gram.shape[1], TILE)


def solution(mesh):
    fits = mesh.shape["dp"] == 2 and mesh.shape["mp"] == 16
    return jax.shard_map(
        fused_body if fits else general_body,
        mesh=mesh,
        in_specs=(
            P(("dp", "mp"), None),
            P("dp", "mp"),
            P("dp", "mp"),
            P("dp", "mp"),
            P("dp", None),
            P("dp", None),
            P("mp"),
        ),
        out_specs=(P("mp", "dp", None), P(None, "mp", None, "dp", None)),
        check_vma=False,
    )
```

```python
import functools

import jax
import jax.numpy as jnp
from jax import lax
from jax.experimental import pallas as pl
from jax.experimental.pallas import tpu as pltpu
from jax.sharding import PartitionSpec as P

TILE = 128
GBLK = 896
MESH = pl.DeviceIdType.MESH
F32 = jnp.float32
BF16 = jnp.bfloat16


def largest_divisor(number, limit):
    return max(d for d in range(1, limit + 1) if number % d == 0)


def fused_kernel(
    scale,
    ratio,
    act_in,
    gate_in,
    up_in,
    hid_in,
    counts_in,
    lengths_in,
    owner_in,
    act_out,
    grad_out,
    counts,
    lengths,
    owner,
    own_raw,
    gate,
    up,
    hid,
    near,
    far,
    xt,
    sc,
    sct,
    wt,
    rb,
    cb,
    part_a,
    recv_a,
    part_g,
    recv_g,
    stage_a,
    stage_g,
    in_sem,
    out_a_sem,
    out_g_sem,
    zs,
    zr,
    fs,
    fr,
    hs,
    hr,
    gs,
    gr,
    as_,
    ar,
):
    g = lax.axis_index("dp")
    me = lax.axis_index("mp")
    z = me // 4
    y = (me // 2) % 2
    x = me % 2
    xy = me % 4
    xn = me + 1 - 2 * x
    yn = me + 2 - 4 * y
    z1 = z + 1 - 2 * (z % 2)
    z2 = (z + 2) % 4
    z3 = 3 - z
    mid = ((z + 1) // 2) % 2
    is_mid = mid == 1
    cap = act_in.shape[0]
    blocks = near.shape[1]

    def place(item, slot_xy):
        return (near, far)[item // 2], (item % 2) * 4 + slot_xy

    def slot_of(item, slot_xy):
        ref, index = place(item, slot_xy)
        return ref.at[index]

    half = blocks // 2
    xy_of_xn = y * 2 + (1 - x)
    xy_of_yn = (1 - y) * 2 + x
    xy_of_d = (1 - y) * 2 + (1 - x)

    loads = [
        pltpu.make_async_copy(counts_in, counts, in_sem.at[4]),
        pltpu.make_async_copy(act_in, own_raw, in_sem.at[0]),
        pltpu.make_async_copy(gate_in, gate, in_sem.at[1]),
        pltpu.make_async_copy(up_in, up, in_sem.at[2]),
        pltpu.make_async_copy(hid_in, hid, in_sem.at[3]),
        pltpu.make_async_copy(lengths_in, lengths, in_sem.at[5]),
        pltpu.make_async_copy(owner_in, owner, in_sem.at[6]),
    ]
    for copy in loads:
        copy.start()

    loads[0].wait()
    loads[1].wait()
    live = counts[0, me]
    row_live = lax.broadcasted_iota(jnp.int32, (cap, TILE), 0) < live

    def put_own(b, carry):
        value = own_raw[:, pl.ds(pl.multiple_of(b * TILE, TILE), TILE)]
        near[xy, b] = jnp.where(row_live, value.astype(F32), 0.0).astype(BF16)
        return carry

    lax.fori_loop(0, blocks, put_own, 0, unroll=8)

    barrier = pltpu.get_barrier_semaphore()
    for other in ((1 - g, me), (g, xn), (g, yn), (g, z1 * 4 + xy)):
        pl.semaphore_signal(barrier, inc=1, device_id=other, device_id_type=MESH)

    @pl.when(is_mid)
    def _():
        pl.semaphore_signal(
            barrier, inc=1, device_id=(g, z3 * 4 + xy), device_id_type=MESH
        )

    pl.semaphore_wait(barrier, 4 + mid)

    def z_copy(src_item, target_z, index, which):
        return pltpu.make_async_remote_copy(
            src_ref=slot_of(src_item, xy), dst_ref=slot_of(which + 1, xy),
            send_sem=zs.at[index], recv_sem=zr.at[which],
            device_id=(g, target_z * 4 + xy), device_id_type=MESH,
        )

    def full_copy(way, item, slot_xy, target):
        slot = slot_of(item, slot_xy)
        return pltpu.make_async_remote_copy(
            src_ref=slot, dst_ref=slot, send_sem=fs.at[way, item], recv_sem=fr.at[way, item],
            device_id=(g, target), device_id_type=MESH,
        )

    def half_copy(way, item, slot_xy, target):
        ref, index = place(item, slot_xy)
        slot = ref.at[index, pl.ds(way * half, half)]
        return pltpu.make_async_remote_copy(
            src_ref=slot, dst_ref=slot, send_sem=hs.at[way, item], recv_sem=hr.at[way, item],
            device_id=(g, target), device_id_type=MESH,
        )

    def send_item(item):
        full_copy(0, item, xy, xn).start()
        full_copy(1, item, xy, yn).start()

    def pass_halves(item):
        full_copy(1, item, xy_of_yn, yn).wait_recv()
        half_copy(0, item, xy_of_yn, xn).start()
        full_copy(0, item, xy_of_xn, xn).wait_recv()
        half_copy(1, item, xy_of_xn, yn).start()

    def take_halves(item):
        half_copy(0, item, xy_of_d, xn).wait_recv()
        half_copy(1, item, xy_of_d, yn).wait_recv()

    z_copy(0, z1, 0, 0).start()
    send_item(0)

    @pl.when(is_mid)
    def _():
        z_copy(0, z3, 1, 1).start()

    for copy in loads[2:]:
        copy.wait()

    within = lax.broadcasted_iota(jnp.int32, (cap, TILE), 0)
    seqs = lengths.shape[1]

    def put_weight(j, offset):
        here = counts[0, j]
        position = within + offset
        own = jnp.ones((cap, TILE), jnp.int32)
        start = jnp.int32(0)
        for k in range(seqs):
            size = lengths[0, k]
            inside = (position >= start) & (position < start + size)
            own = jnp.where(inside, size, own)
            start = start + size
        own = jnp.maximum(own, 1).astype(F32)
        wt[pl.ds(pl.multiple_of(j * cap, cap), cap), :] = jnp.where(
            within < here, ratio / own, 0.0
        )
        return offset + here

    lax.fori_loop(0, counts.shape[1], put_weight, jnp.int32(0))

    per = sc.shape[1]
    span = GBLK // TILE
    rows = gate.shape[0]
    chunk = 64

    def scaled_block(n, carry):
        m = n // span
        for c in range(rows // chunk):
            rs = slice(c * chunk, (c + 1) * chunk)
            cols = pl.ds(pl.multiple_of(n * TILE, TILE), TILE)
            a = gate[rs, cols].astype(F32)
            b = up[rs, cols].astype(F32)
            h = hid[rs, cols].astype(F32)
            w = wt[rs, :]
            q = 0.5 * jnp.tanh(0.5 * a) + 0.5
            hq = h * q
            gate_grad = hq * b * (1.0 + a * (1.0 - q))
            up_grad = hq * a
            sc[0, m, n % span, rs, :] = (gate_grad * w).astype(BF16)
            sc[1, m, n % span, rs, :] = (up_grad * w).astype(BF16)
        for e in range(2):
            sct[e, m, n % span] = sc[e, m, n % span].T
        return carry

    lax.fori_loop(0, per * span, scaled_block, 0)

    z_copy(0, z1, 0, 0).wait_recv()
    send_item(1)

    @pl.when(is_mid)
    def _():
        z_copy(1, z3, 2, 2).start()

    pass_halves(0)

    pairs = [(i, j) for i in range(span) for j in range(i, span)]
    other_rows = pl.ds(pl.multiple_of(64 * (1 - g), 64), 64)
    own_rows = pl.ds(pl.multiple_of(64 * g, 64), 64)

    def grad_send(q):
        return pltpu.make_async_remote_copy(
            src_ref=part_g.at[q, :, other_rows], dst_ref=recv_g.at[q],
            send_sem=gs.at[q], recv_sem=gr.at[q],
            device_id=(1 - g, me), device_id_type=MESH,
        )

    def grad_tiles(q, carry):
        e = q // per
        m = q % per
        for k, (i, j) in enumerate(pairs):
            tile = jnp.dot(sct[e, m, i], sc[e, m, j], preferred_element_type=F32)
            part_g[q, k] = (tile * scale).astype(BF16)
        grad_send(q).start()
        return carry

    lax.fori_loop(0, 2 * per, grad_tiles, 0)

    z_copy(2, z1, 0, 1).wait_recv()
    send_item(2)

    @pl.when(is_mid)
    def _():
        z_copy(2, z1, 3, 1).start()

    pass_halves(1)

    z_copy(3, z1, 0, 2).wait_recv()
    send_item(3)

    @pl.when(is_mid)
    def _():
        z_copy(3, z1, 4, 2).start()

    tiles = owner.shape[0]

    def put_coords(k, carry):
        t = owner[k]
        r = jnp.int32(0)
        step = 1
        while step * 2 < blocks:
            step *= 2
        while step:
            cand = r + step
            begin = cand * blocks - (cand * (cand - 1)) // 2
            r = jnp.where((cand < blocks) & (t >= begin), cand, r)
            step //= 2
        rb[k] = r
        cb[k] = t - (r * blocks - (r * (r - 1)) // 2) + r
        return carry

    lax.fori_loop(0, tiles, put_coords, 0)

    def grad_out_copy(q):
        return pltpu.make_async_copy(
            stage_g.at[q], grad_out.at[q // per, q % per], out_g_sem.at[q]
        )

    def grad_finish(q, carry):
        grad_send(q).wait()
        for k in range(len(pairs)):
            total = part_g[q, k, own_rows].astype(F32) + recv_g[q, k].astype(F32)
            stage_g[q, k] = total.astype(BF16)
        grad_out_copy(q).start()
        return carry

    take_halves(0)
    take_halves(1)

    group = 8

    def transpose_half(which):
        def one(b, carry):
            block = (near, far)[which][:, b].reshape(group * cap, TILE)
            xt[b, :, which * TILE : (which + 1) * TILE] = block.T
            return carry

        lax.fori_loop(0, blocks, one, 0, unroll=4)

    pass_halves(2)
    lax.fori_loop(0, 2 * per, grad_finish, 0)
    transpose_half(0)
    pass_halves(3)
    take_halves(2)
    take_halves(3)
    transpose_half(1)

    chunks = part_a.shape[0]
    width = part_a.shape[1]

    def act_send(n):
        return pltpu.make_async_remote_copy(
            src_ref=part_a.at[n, :, other_rows], dst_ref=recv_a.at[n],
            send_sem=as_.at[n], recv_sem=ar.at[n],
            device_id=(1 - g, me), device_id_type=MESH,
        )

    def act_out_copy(n):
        return pltpu.make_async_copy(
            stage_a.at[n], act_out.at[pl.ds(n * width, width)], out_a_sem.at[n]
        )

    def act_tiles(n, carry):
        for i in range(width):
            k = n * width + i
            left = xt[rb[k]]
            c = cb[k]
            right = jnp.concatenate(
                [ref[:, c].reshape(TILE, TILE) for ref in (near, far)], axis=0
            )
            tile = jnp.dot(left, right, preferred_element_type=F32)
            part_a[n, i] = (tile * scale).astype(BF16)
        act_send(n).start()
        return carry

    def act_finish(n, carry):
        act_send(n).wait()
        for i in range(width):
            total = part_a[n, i, own_rows].astype(F32) + recv_a[n, i].astype(F32)
            stage_a[n, i] = total.astype(BF16)
        act_out_copy(n).start()
        return carry

    def act_both(n, carry):
        act_tiles(n, carry)
        act_finish(n - 2, carry)
        return carry

    lax.fori_loop(0, 2, act_tiles, 0)
    lax.fori_loop(2, chunks, act_both, 0)
    lax.fori_loop(chunks - 2, chunks, act_finish, 0)

    z_copy(0, z1, 0, 0).wait_send()

    @pl.when(is_mid)
    def _():
        z_copy(0, z3, 1, 1).wait_send()
        z_copy(1, z3, 2, 2).wait_send()
        z_copy(2, z1, 3, 1).wait_send()
        z_copy(3, z1, 4, 2).wait_send()

    for item in range(4):
        full_copy(0, item, xy, xn).wait_send()
        full_copy(1, item, xy, yn).wait_send()
        half_copy(0, item, xy_of_yn, xn).wait_send()
        half_copy(1, item, xy_of_xn, yn).wait_send()

    def wait_grad_out(q, carry):
        grad_out_copy(q).wait()
        return carry

    def wait_act_out(n, carry):
        act_out_copy(n).wait()
        return carry

    lax.fori_loop(0, 2 * per, wait_grad_out, 0)
    lax.fori_loop(0, chunks, wait_act_out, 0)


def fused_body(acts, gate, up, hid, counts, lengths, owner):
    cap, width = acts.shape
    slots = 16
    rows = slots * cap
    live_total = rows - 2 * cap
    blocks = width // TILE
    tiles = owner.shape[0]
    per = gate.shape[1] // GBLK
    span = GBLK // TILE
    pairs = span * (span + 1) // 2
    chunk = largest_divisor(tiles, 10)
    chunks = tiles // chunk
    anywhere = pl.BlockSpec(memory_space=pl.ANY)
    in_hbm = pl.BlockSpec(memory_space=pltpu.HBM)
    dma = pltpu.SemaphoreType.DMA
    kernel = functools.partial(
        fused_kernel, 1.0 / (2 * live_total), live_total / lengths.shape[1]
    )
    return pl.pallas_call(
        kernel,
        out_shape=(
            jax.ShapeDtypeStruct((tiles, TILE // 2, TILE), BF16),
            jax.ShapeDtypeStruct((2, per, pairs, TILE // 2, TILE), BF16),
        ),
        in_specs=[in_hbm] * 7,
        out_specs=(anywhere, anywhere),
        scratch_shapes=[
            pltpu.SMEM(counts.shape, jnp.int32),
            pltpu.SMEM(lengths.shape, jnp.int32),
            pltpu.SMEM(owner.shape, jnp.int32),
            pltpu.VMEM((cap, width), BF16),
            pltpu.VMEM(gate.shape, BF16),
            pltpu.VMEM(gate.shape, BF16),
            pltpu.VMEM(gate.shape, BF16),
            pltpu.VMEM((slots // 2, blocks, cap, TILE), BF16),
            pltpu.VMEM((slots // 2, blocks, cap, TILE), BF16),
            pltpu.VMEM((blocks, TILE, rows), BF16),
            pltpu.VMEM((2, per, span, rows, TILE), BF16),
            pltpu.VMEM((2, per, span, TILE, rows), BF16),
            pltpu.VMEM((rows, TILE), F32),
            pltpu.SMEM((tiles,), jnp.int32),
            pltpu.SMEM((tiles,), jnp.int32),
            pltpu.VMEM((chunks, chunk, TILE, TILE), BF16),
            pltpu.VMEM((chunks, chunk, TILE // 2, TILE), BF16),
            pltpu.VMEM((2 * per, pairs, TILE, TILE), BF16),
            pltpu.VMEM((2 * per, pairs, TILE // 2, TILE), BF16),
            pltpu.VMEM((chunks, chunk, TILE // 2, TILE), BF16),
            pltpu.VMEM((2 * per, pairs, TILE // 2, TILE), BF16),
            dma((7,)),
            dma((chunks,)),
            dma((2 * per,)),
            dma((5,)),
            dma((3,)),
            dma((2, 4)),
            dma((2, 4)),
            dma((2, 4)),
            dma((2, 4)),
            dma((2 * per,)),
            dma((2 * per,)),
            dma((chunks,)),
            dma((chunks,)),
        ],
        compiler_params=pltpu.CompilerParams(
            collective_id=0, has_side_effects=True, vmem_limit_bytes=36 * 2**20
        ),
        cost_estimate=pl.CostEstimate(
            flops=4 * 10**9, bytes_accessed=12 * 10**6, transcendentals=10**6
        ),
    )(
        *(
            pltpu.with_memory_space_constraint(array, pltpu.HBM)
            for array in (acts, gate, up, hid, counts, lengths, owner)
        )
    )


def tile_coords(tile_ids, block_count):
    block_ids = jnp.arange(block_count, dtype=jnp.int32)
    starts = block_ids * block_count - block_ids * (block_ids - 1) // 2
    row_block = jnp.sum((tile_ids[:, None] >= starts[None, :]).astype(jnp.int32), axis=1) - 1
    first_tile = jnp.sum(
        jnp.where(block_ids[None, :] == row_block[:, None], starts[None, :], 0), axis=1
    )
    return row_block, tile_ids - first_tile + row_block


def sums_before(values):
    ids = jnp.arange(values.shape[0], dtype=jnp.int32)
    return jnp.sum(jnp.where(ids[None, :] < ids[:, None], values[None, :], 0), axis=1)


def slot_weights(counts, lengths, capacity, live_total):
    slot_ids = jnp.arange(counts.shape[0] * capacity, dtype=jnp.int32)
    device_ids = jnp.arange(counts.shape[0], dtype=jnp.int32)
    match = (slot_ids // capacity)[:, None] == device_ids[None, :]
    within = slot_ids % capacity
    live_mask = within < jnp.sum(jnp.where(match, counts[None, :], 0), axis=1)
    position = within + jnp.sum(jnp.where(match, sums_before(counts)[None, :], 0), axis=1)
    begins = sums_before(lengths)
    inside = (position[:, None] >= begins[None, :]) & (
        position[:, None] < (begins + lengths)[None, :]
    )
    own = jnp.maximum(jnp.sum(jnp.where(inside, lengths[None, :], 0), axis=1), 1)
    ratio = live_total / lengths.shape[0]
    return live_mask, jnp.where(live_mask, ratio / own.astype(F32), 0.0)


def general_body(acts, gate_pre, up_pre, hidden_grad, counts, lengths, owner):
    mp_size = lax.axis_size("mp")
    dp_size = lax.axis_size("dp")
    capacity = acts.shape[0]
    live_total = mp_size * capacity - 2 * capacity
    scale = 1.0 / (dp_size * live_total)
    live_mask, weight = slot_weights(counts[0], lengths[0], capacity, live_total)
    row_block, col_block = tile_coords(owner, acts.shape[1] // TILE)
    a = gate_pre.astype(F32)
    b = up_pre.astype(F32)
    h = hidden_grad.astype(F32)
    q = jax.nn.sigmoid(a)
    w = weight[:, None]
    scaled = (
        (h * b * q * (1.0 + a * (1.0 - q)) * w).astype(BF16),
        (h * a * q * w).astype(BF16),
    )
    per = gate_pre.shape[1] // GBLK
    span = GBLK // TILE
    pieces = []
    for e in range(2):
        for block in range(per):
            for strip in range(span):
                first = block * GBLK + strip * TILE
                product = lax.dot_general(
                    scaled[e][:, first : first + TILE],
                    scaled[e][:, first : (block + 1) * GBLK],
                    (((0,), (0,)), ((), ())),
                    preferred_element_type=F32,
                )
                product = (product * scale).astype(BF16)
                pieces.append(product.reshape(TILE, span - strip, TILE).transpose(1, 0, 2))
    grad_tiles = jnp.concatenate(pieces, axis=0)
    mine = jnp.sum(
        jnp.where(
            jnp.arange(mp_size) == lax.axis_index("mp"), counts[0], 0
        )
    )
    kept = jnp.where(jnp.arange(capacity)[:, None] < mine, acts, 0)
    rows = lax.all_gather(kept, "mp", axis=0, tiled=True)

    def one_tile(pair):
        left = lax.dynamic_slice_in_dim(rows, pair[0] * TILE, TILE, 1)
        right = lax.dynamic_slice_in_dim(rows, pair[1] * TILE, TILE, 1)
        product = lax.dot_general(
            left, right, (((0,), (0,)), ((), ())), preferred_element_type=F32
        )
        return (product * scale).astype(BF16)

    act_tiles = lax.map(one_tile, (row_block, col_block))
    act_gram = lax.psum_scatter(act_tiles, "dp", scatter_dimension=1, tiled=True)
    grad_gram = lax.psum_scatter(grad_tiles, "dp", scatter_dimension=1, tiled=True)
    return act_gram, grad_gram.reshape(2, per, -1, grad_gram.shape[1], TILE)


def solution(mesh):
    fits = mesh.shape["dp"] == 2 and mesh.shape["mp"] == 16
    return jax.shard_map(
        fused_body if fits else general_body,
        mesh=mesh,
        in_specs=(
            P(("dp", "mp"), None),
            P("dp", "mp"),
            P("dp", "mp"),
            P("dp", "mp"),
            P("dp", None),
            P("dp", None),
            P("mp"),
        ),
        out_specs=(P("mp", "dp", None), P(None, "mp", None, "dp", None)),
        check_vma=False,
    )
```
